32 devices in a mesh: slab: 8 (over z, y), term: 4 (over x, core).
Axes of the slice: x: 2, y: 2, z: 4, core: 2. Of those that a mesh axis runs over, the one named last changes fastest.
Arguments:
- right_side: float32 [84, 16, 128, 128], P('term', 'slab'), may hold values from -24 to 24
- mean_cond: float32 [16, 128, 128], P('slab', 'term'), may hold values from 2 to 4
- cond_terms: float32 [6, 16, 128, 128], P(None, 'slab', 'term'), may hold values from -0.3 to 0.3
Outputs:
- solution: float32 [84, 16, 128, 128], P('term', 'slab')
- residual: float32 [84, 16, 128, 128], P('term', 'slab')
The draws below stay inside these ranges and needn't reach their ends.
All inputs are finite; a program needn't handle non-finite values.
Results may differ from the reference program's by a relative error of at most 0.00013.
Values sent between devices are 32-bit elements; how exact they have to be, the bound alone decides.
A program may use at most 64 MiB of HBM per device.

```python
import math
import jax
import jax.numpy as jnp
from jax import lax

DIM = 6
DEG = 3
P_SIZE = 84
ITERS = 2
NX = 128
NY = 128
NZ = 16


def block_levels(rng, shape, split, least, high):
    def one(dim, shards_of):
        draws = jax.random.uniform(jax.random.fold_in(jax.random.fold_in(rng, 6), dim), (shards_of,), jnp.float32, least / len(split), high / len(split))
        return jnp.repeat(jnp.exp(draws), shape[dim] // shards_of).reshape((-1,) + (1,) * (len(shape) - dim - 1))

    gain = one(*split[0])
    for cut in split[1:]:
        gain = gain * one(*cut)
    return gain


def bell_draw(own_key, extent, scale, bound, cuts=(), kind=jnp.bfloat16):
    drawn = scale * jax.random.normal(own_key, extent, jnp.float32)
    if cuts:
        drawn = drawn * block_levels(own_key, extent, cuts, -0.22, 0.18)
    return jnp.clip(drawn, -bound, bound).astype(kind)


def setup_inputs(seed: int = 0) -> dict:
    splits = jax.random.split(jax.random.key(seed), 4)
    right_side = bell_draw(splits[0], (P_SIZE, NZ, NY, NX), 4.0, 24.0, ((0, 4), (1, 8)), jnp.float32)
    mean_cond = jnp.clip(2.0 + 2.0 * jax.random.uniform(splits[1], (NZ, NY, NX), jnp.float32) ** block_levels(splits[1], (NZ, NY, NX), ((0, 8), (1, 4)), -0.2, 0.2), 2.0, 4.0)
    cond_terms = jnp.clip(jax.random.uniform(splits[2], (DIM, NZ, NY, NX), jnp.float32, -0.3, 0.3) * block_levels(splits[2], (DIM, NZ, NY, NX), ((1, 8), (2, 4)), -0.4, 0.0), -0.3, 0.3)
    return {"right_side": right_side, "mean_cond": mean_cond, "cond_terms": cond_terms}


lower_edge = 2.0
upper_edge = 72.0

def compositions(degree_sum, slots_left):
    if slots_left == 1:
        return [[degree_sum]]
    listing = []
    for leading in range(degree_sum, -1, -1):
        for remainder in compositions(degree_sum - leading, slots_left - 1):
            listing.append([leading] + remainder)
    return listing

def galerkin_tables(variables, degree):
    indices = []
    for degree_level in range(degree + 1):
        indices.extend(compositions(degree_level, variables))
    count = len(indices)
    tables = []
    for variable in range(variables):
        rows_list = []
        for row in range(count):
            first = indices[row]
            entries = []
            for col in range(count):
                second = indices[col]
                agreeing = all((first[m] == second[m] for m in range(variables) if m != variable))
                value = 0.0
                if agreeing and abs(first[variable] - second[variable]) == 1:
                    higher = max(first[variable], second[variable])
                    value = higher / math.sqrt(4.0 * higher * higher - 1.0)
                entries.append(value)
            rows_list.append(entries)
        tables.append(rows_list)
    return tables

def laplace(extended, field):
    beside = extended[:, 2:, 1:-1, 1:-1] + extended[:, :-2, 1:-1, 1:-1]
    beside = beside + extended[:, 1:-1, 2:, 1:-1] + extended[:, 1:-1, :-2, 1:-1]
    beside = beside + extended[:, 1:-1, 1:-1, 2:] + extended[:, 1:-1, 1:-1, :-2]
    return 6.0 * field - beside

def coupling(lap_field, mean_cond, cond_terms, tables):
    flat = lap_field.reshape(lap_field.shape[0], -1)
    result = mean_cond.reshape(1, -1) * flat
    terms_flat = cond_terms.reshape(cond_terms.shape[0], -1)
    for variable in range(cond_terms.shape[0]):
        mixed = jnp.dot(tables[variable], flat, precision=lax.Precision.HIGHEST, preferred_element_type=jnp.float32)
        result = result + terms_flat[variable][None, :] * mixed
    return result.reshape(lap_field.shape)

def chebyshev(right_side, apply_operator):
    center_value = 0.5 * (upper_edge + lower_edge)
    half_width = 0.5 * (upper_edge - lower_edge)
    sigma_value = center_value / half_width
    rho_now = 1.0 / sigma_value
    residual = right_side
    direction = right_side / center_value
    solution = jnp.zeros_like(right_side)
    for iteration in range(ITERS):
        solution = solution + direction
        residual = residual - apply_operator(direction)
        rho_next = 1.0 / (2.0 * sigma_value - rho_now)
        if iteration + 1 < ITERS:
            direction = rho_next * rho_now * direction + 2.0 * rho_next / half_width * residual
        rho_now = rho_next
    return (solution, residual)

def reference(right_side, mean_cond, cond_terms):
    tables = jnp.asarray(galerkin_tables(DIM, DEG), jnp.float32)

    def apply_operator(field):
        extended = jnp.pad(field, ((0, 0), (1, 1), (1, 1), (1, 1)))
        lap_field = laplace(extended, field)

        def per_plane(pieces):
            return coupling(pieces[0], pieces[1], pieces[2], tables)
        planes = lax.map(per_plane, (jnp.moveaxis(lap_field, 1, 0), mean_cond, jnp.moveaxis(cond_terms, 1, 0)))
        return jnp.moveaxis(planes, 0, 1)
    solution, residual = chebyshev(right_side, apply_operator)
    return (solution, residual)
```

```python
import functools
import math

import jax
import jax.numpy as jnp
from jax import lax
from jax.experimental import pallas as pl
from jax.experimental.pallas import tpu as pltpu
from jax.sharding import PartitionSpec as P

DIM = 6
DEG = 3
ITERS = 2

lower_edge = 2.0
upper_edge = 72.0


def compositions(degree_sum, slots_left):
    if slots_left == 1:
        return [[degree_sum]]
    listing = []
    for leading in range(degree_sum, -1, -1):
        for remainder in compositions(degree_sum - leading, slots_left - 1):
            listing.append([leading] + remainder)
    return listing


def galerkin_entries(variables, degree):
    indices = []
    for degree_level in range(degree + 1):
        indices.extend(tuple(c) for c in compositions(degree_level, variables))
    place = {index: i for i, index in enumerate(indices)}
    rows = []
    for index in indices:
        per_variable = []
        for variable in range(variables):
            entries = []
            for step in (-1, 1):
                other = list(index)
                other[variable] += step
                col = place.get(tuple(other))
                if col is not None:
                    higher = max(index[variable], other[variable])
                    entries.append((col, higher / math.sqrt(4.0 * higher * higher - 1.0)))
            per_variable.append(entries)
        rows.append(per_variable)
    return rows


def kernel(
    dims,
    b_hbm, mean_hbm, cond_hbm,
    sol_hbm, res_hbm,
    bufb, bufd, lap, r1, sol, cond,
    rows_out, rows_in,
    local_sem, b_send, b_recv, c_send, c_recv, z_send, z_recv, r_send, r_recv, o_send, o_recv,
):
    slabs, nt, tp, zp, rb, terms = dims
    planes = 2 * zp
    pairs = slabs // 2
    bands = 2 * nt
    first, last = 8, 8 + rb
    s = lax.axis_index("slab")
    t = lax.axis_index("term")
    q = s // 2
    h = s % 2
    g = 2 * t + (h + t) % 2

    def band_of(hh, tt):
        return 2 * tt + (hh + tt) % 2

    def owner(band):
        tt = band // 2
        return (band % 2 + tt) % 2, tt

    def dev(qq, hh, tt):
        return {"slab": 2 * qq + hh, "term": tt}

    offsets = [(dh, dt) for dh in range(2) for dt in range(nt) if (dh, dt) != (0, 0)]

    def partner(sign, dh, dt):
        return (h + dh) % 2, (t + sign * dt + nt) % nt

    barrier = pltpu.get_barrier_semaphore()
    for dh, dt in offsets:
        hh, tt = partner(1, dh, dt)
        pl.semaphore_signal(barrier, inc=1, device_id=dev(q, hh, tt), device_id_type=pl.DeviceIdType.MESH)

    @pl.when(q > 0)
    def _():
        pl.semaphore_signal(barrier, inc=1, device_id=dev(q - 1, h, t), device_id_type=pl.DeviceIdType.MESH)

    @pl.when(q < pairs - 1)
    def _():
        pl.semaphore_signal(barrier, inc=1, device_id=dev(q + 1, h, t), device_id_type=pl.DeviceIdType.MESH)

    below = (q + pairs - 1) // pairs
    above = (2 * pairs - 2 - q) // pairs
    pl.semaphore_wait(barrier, len(offsets) + below + above)

    def remote(src, dst, send, recv, device):
        return pltpu.make_async_remote_copy(
            src_ref=src, dst_ref=dst, send_sem=send, recv_sem=recv,
            device_id=device, device_id_type=pl.DeviceIdType.MESH,
        )

    def band_rows(band):
        return pl.ds(pl.multiple_of(band * rb, 8), rb)

    own_dst = bufb.at[pl.ds(t * tp, tp), pl.ds(1 + h * zp, zp), pl.ds(first, rb), :]
    b_copies = []
    for n, (dh, dt) in enumerate(offsets):
        hh, tt = partner(1, dh, dt)
        copy = remote(
            b_hbm.at[:, :, band_rows(band_of(hh, tt)), :], own_dst,
            b_send.at[n], b_recv.at[n], dev(q, hh, tt),
        )
        copy.start()
        b_copies.append(copy)
    own_b = pltpu.make_async_copy(b_hbm.at[:, :, band_rows(g), :], own_dst, local_sem.at[0])
    own_b.start()

    def half(hh):
        return pl.ds(pl.multiple_of(rb * ((hh + t) % 2), 8), rb)

    my_planes = pl.ds(h * zp, zp)
    other = dev(q, 1 - h, t)
    c_copies = [
        remote(cond_hbm.at[:, :, half(1 - h), :], cond.at[pl.ds(0, DIM), my_planes], c_send.at[0], c_recv.at[0], other),
        remote(mean_hbm.at[:, half(1 - h), :], cond.at[DIM, my_planes], c_send.at[1], c_recv.at[1], other),
    ]
    own_c = [
        pltpu.make_async_copy(cond_hbm.at[:, :, half(h), :], cond.at[pl.ds(0, DIM), my_planes], local_sem.at[1]),
        pltpu.make_async_copy(mean_hbm.at[:, half(h), :], cond.at[DIM, my_planes], local_sem.at[2]),
    ]
    for copy in c_copies + own_c:
        copy.start()

    def clear(plane):
        def body(j, carry):
            zero = jnp.zeros((rb, 128), jnp.float32)
            bufb[j, plane, first:last, :] = zero
            bufd[j, plane, first:last, :] = zero
            return carry
        lax.fori_loop(0, terms, body, 0)

    @pl.when(q == 0)
    def _():
        clear(0)

    @pl.when(q == pairs - 1)
    def _():
        clear(planes + 1)

    @pl.when(g == 0)
    def _():
        rows_in[0, 0] = jnp.zeros(rows_in.shape[2:], jnp.float32)
        rows_in[1, 0] = jnp.zeros(rows_in.shape[2:], jnp.float32)

    @pl.when(g == bands - 1)
    def _():
        rows_in[0, 1] = jnp.zeros(rows_in.shape[2:], jnp.float32)
        rows_in[1, 1] = jnp.zeros(rows_in.shape[2:], jnp.float32)

    def z_copy(step, buf, hh, part, at, size):
        slot = step * bands + hh * nt + part
        return remote(
            buf.at[pl.ds(at, size), 1 + (planes - 1) * hh, pl.ds(first, rb), :],
            buf.at[pl.ds(at, size), (planes + 1) * (1 - hh), pl.ds(first, rb), :],
            z_send.at[slot], z_recv.at[slot], dev(q - 1 + 2 * hh, h, t),
        )

    def z_sends(hh):
        target = q - 1 + 2 * hh
        return jnp.logical_and(target >= 0, target < pairs)

    def z_receives(hh):
        source = q + 1 - 2 * hh
        return jnp.logical_and(source >= 0, source < pairs)

    def forward(hh, tt):
        @pl.when(z_sends(hh))
        def _():
            z_copy(0, bufb, hh, tt, tt * tp, tp).start()

    own_b.wait()
    forward(h, t)
    for n, (dh, dt) in enumerate(offsets):
        b_copies[n].wait_recv()
        hh, tt = partner(-1, dh, dt)
        forward(hh, tt)

    def row_copies(step):
        up_h, up_t = owner(lax.rem(g + bands - 1, bands))
        down_h, down_t = owner(lax.rem(g + 1, bands))
        up = remote(rows_out.at[step, 0], rows_in.at[step, 1], r_send.at[step, 0], r_recv.at[step, 1], dev(q, up_h, up_t))
        down = remote(rows_out.at[step, 1], rows_in.at[step, 0], r_send.at[step, 1], r_recv.at[step, 0], dev(q, down_h, down_t))
        return up, down

    def pack(step, buf):
        def body(jj, carry):
            for a in range(2):
                for p in range(planes):
                    at = planes * a + p
                    rows_out[step, 0, jj, at:at + 1, :] = buf[2 * jj + a, p + 1, first:first + 1, :]
                    rows_out[step, 1, jj, at:at + 1, :] = buf[2 * jj + a, p + 1, last - 1:last, :]
            return carry
        lax.fori_loop(0, terms // 2, body, 0)

    def start_rows(step):
        up, down = row_copies(step)

        @pl.when(g > 0)
        def _():
            up.start()

        @pl.when(g < bands - 1)
        def _():
            down.start()

    def wait_rows(step):
        up, down = row_copies(step)

        @pl.when(g > 0)
        def _():
            down.wait_recv()
            up.wait_send()

        @pl.when(g < bands - 1)
        def _():
            up.wait_recv()
            down.wait_send()

    def laplacian(step, buf):
        lane = lax.broadcasted_iota(jnp.int32, (planes, rb, 128), 2)
        inner = slice(1, planes + 1)

        def body(jj, carry):
            for a in range(2):
                j = 2 * jj + a
                for p in range(planes):
                    at = planes * a + p
                    buf[j, p + 1, first - 1:first, :] = rows_in[step, 0, jj, at:at + 1, :]
                    buf[j, p + 1, last:last + 1, :] = rows_in[step, 1, jj, at:at + 1, :]
            for a in range(2):
                j = 2 * jj + a
                field = buf[j, inner, first:last, :]
                beside = buf[j, 2:planes + 2, first:last, :] + buf[j, 0:planes, first:last, :]
                beside = beside + buf[j, inner, first + 1:last + 1, :] + buf[j, inner, first - 1:last - 1, :]
                after = jnp.where(lane == 127, 0.0, pltpu.roll(field, 127, 2))
                before = jnp.where(lane == 0, 0.0, pltpu.roll(field, 1, 2))
                lap[j] = 6.0 * field - (beside + after + before)
            return carry
        lax.fori_loop(0, terms // 2, body, 0)

    table = galerkin_entries(DIM, DEG)

    def coupled(finish):
        def body(p, carry):
            factors = [cond[k, p] for k in range(DIM)]
            mean = cond[DIM, p]
            for i in range(terms):
                total = mean * lap[i, p]
                for k in range(DIM):
                    mixed = None
                    for col, value in table[i][k]:
                        part = value * lap[col, p]
                        mixed = part if mixed is None else mixed + part
                    if mixed is not None:
                        total = total + factors[k] * mixed
                finish(i, p, total)
            return carry
        lax.fori_loop(0, planes, body, 0)

    center = 0.5 * (upper_edge + lower_edge)
    half_width = 0.5 * (upper_edge - lower_edge)
    sigma = center / half_width
    rho = 1.0 / sigma
    rho_next = 1.0 / (2.0 * sigma - rho)

    def finish_first(i, p, total):
        b = bufb[i, p + 1, first:last, :]
        residual = b - (1.0 / center) * total
        start = (1.0 / center) * b
        direction = (rho_next * rho) * start + (2.0 * rho_next / half_width) * residual
        r1[i, p] = residual
        bufd[i, p + 1, first:last, :] = direction
        sol[i, p] = start + direction

    def finish_second(i, p, total):
        r1[i, p] = r1[i, p] - total

    def out_copies(which, src, dst):
        copies = []
        for n, (dh, dt) in enumerate(offsets):
            hh, tt = partner(1, dh, dt)
            slot = which * len(offsets) + n
            copies.append(remote(
                src.at[pl.ds(tt * tp, tp), pl.ds(hh * zp, zp)],
                dst.at[:, :, band_rows(g), :],
                o_send.at[slot], o_recv.at[slot], dev(q, hh, tt),
            ))
        own = pltpu.make_async_copy(
            src.at[pl.ds(t * tp, tp), pl.ds(h * zp, zp)], dst.at[:, :, band_rows(g), :], local_sem.at[3 + which])
        return copies, own

    pack(0, bufb)
    start_rows(0)
    for copy in own_c:
        copy.wait()
    for copy in c_copies:
        copy.wait()
    for hh in range(2):
        for tt in range(nt):
            @pl.when(z_receives(hh))
            def _(hh=hh, tt=tt):
                z_copy(0, bufb, hh, tt, tt * tp, tp).wait_recv()
    wait_rows(0)
    laplacian(0, bufb)
    coupled(finish_first)

    pack(1, bufd)
    start_rows(1)
    for hh in range(2):
        @pl.when(z_sends(hh))
        def _(hh=hh):
            z_copy(1, bufd, hh, 0, 0, terms).start()
    sol_copies, sol_own = out_copies(0, sol, sol_hbm)
    for copy in sol_copies:
        copy.start()
    sol_own.start()
    for hh in range(2):
        @pl.when(z_receives(hh))
        def _(hh=hh):
            z_copy(1, bufd, hh, 0, 0, terms).wait_recv()
    wait_rows(1)
    laplacian(1, bufd)
    coupled(finish_second)
    res_copies, res_own = out_copies(1, r1, res_hbm)
    for copy in res_copies:
        copy.start()
    res_own.start()

    for copy in b_copies:
        copy.wait_send()
    for hh in range(2):
        @pl.when(z_sends(hh))
        def _(hh=hh):
            for tt in range(nt):
                z_copy(0, bufb, hh, tt, tt * tp, tp).wait_send()
            z_copy(1, bufd, hh, 0, 0, terms).wait_send()
    sol_own.wait()
    for copy in sol_copies:
        copy.wait()
    res_own.wait()
    for copy in res_copies:
        copy.wait()


def solution(mesh):
    slabs, nt = mesh.shape["slab"], mesh.shape["term"]

    def shards(right_side, mean_cond, cond_terms):
        tp, zp, ny, nx = right_side.shape
        terms = tp * nt
        rb = ny // (2 * nt)
        planes = 2 * zp
        partners = 2 * nt - 1
        dims = (slabs, nt, tp, zp, rb, terms)
        any_space = pl.BlockSpec(memory_space=pl.ANY)
        return pl.pallas_call(
            functools.partial(kernel, dims),
            out_shape=[jax.ShapeDtypeStruct(right_side.shape, jnp.float32)] * 2,
            in_specs=[any_space] * 3,
            out_specs=[any_space] * 2,
            scratch_shapes=[
                pltpu.VMEM((terms, planes + 2, rb + 16, nx), jnp.float32),
                pltpu.VMEM((terms, planes + 2, rb + 16, nx), jnp.float32),
                pltpu.VMEM((terms, planes, rb, nx), jnp.float32),
                pltpu.VMEM((terms, planes, rb, nx), jnp.float32),
                pltpu.VMEM((terms, planes, rb, nx), jnp.float32),
                pltpu.VMEM((DIM + 1, planes, rb, nx), jnp.float32),
                pltpu.VMEM((2, 2, terms // 2, 2 * planes, nx), jnp.float32),
                pltpu.VMEM((2, 2, terms // 2, 2 * planes, nx), jnp.float32),
                pltpu.SemaphoreType.DMA((5,)),
                pltpu.SemaphoreType.DMA((partners,)),
                pltpu.SemaphoreType.DMA((partners,)),
                pltpu.SemaphoreType.DMA((2,)),
                pltpu.SemaphoreType.DMA((2,)),
                pltpu.SemaphoreType.DMA((4 * nt,)),
                pltpu.SemaphoreType.DMA((4 * nt,)),
                pltpu.SemaphoreType.DMA((2, 2)),
                pltpu.SemaphoreType.DMA((2, 2)),
                pltpu.SemaphoreType.DMA((2 * partners,)),
                pltpu.SemaphoreType.DMA((2 * partners,)),
            ],
            compiler_params=pltpu.CompilerParams(
                collective_id=0, has_side_effects=True, vmem_limit_bytes=48 * 2**20
            ),
        )(right_side, mean_cond, cond_terms)

    placed = (P("term", "slab", None, None), P("slab", "term", None), P(None, "slab", "term", None))
    return jax.shard_map(
        shards,
        mesh=mesh,
        in_specs=placed,
        out_specs=(P("term", "slab", None, None), P("term", "slab", None, None)),
        check_vma=False,
    )
```

```python
import functools
import math

import jax
import jax.numpy as jnp
from jax import lax
from jax.experimental import pallas as pl
from jax.experimental.pallas import tpu as pltpu
from jax.sharding import PartitionSpec as P

DIM = 6
DEG = 3
ITERS = 2

lower_edge = 2.0
upper_edge = 72.0


def compositions(degree_sum, slots_left):
    if slots_left == 1:
        return [[degree_sum]]
    listing = []
    for leading in range(degree_sum, -1, -1):
        for remainder in compositions(degree_sum - leading, slots_left - 1):
            listing.append([leading] + remainder)
    return listing


def galerkin_entries(variables, degree):
    indices = []
    for degree_level in range(degree + 1):
        indices.extend(tuple(c) for c in compositions(degree_level, variables))
    place = {index: i for i, index in enumerate(indices)}
    rows = []
    for index in indices:
        per_variable = []
        for variable in range(variables):
            entries = []
            for step in (-1, 1):
                other = list(index)
                other[variable] += step
                col = place.get(tuple(other))
                if col is not None:
                    higher = max(index[variable], other[variable])
                    entries.append((col, higher / math.sqrt(4.0 * higher * higher - 1.0)))
            per_variable.append(entries)
        rows.append(per_variable)
    return rows


def kernel(
    dims,
    b_hbm, mean_hbm, cond_hbm,
    sol_hbm, res_hbm,
    bufb, bufd, lap, r1, sol, cond,
    rows_out, rows_in,
    local_sem, b_send, b_recv, c_send, c_recv, z_send, z_recv, r_send, r_recv, o_send, o_recv,
):
    slabs, nt, tp, rb, terms = dims
    pairs = slabs // 2
    bands = 2 * nt
    first, last = 8, 8 + rb
    s = lax.axis_index("slab")
    t = lax.axis_index("term")
    q = s // 2
    h = s % 2
    g = 2 * t + (h + t) % 2

    def band_of(hh, tt):
        return 2 * tt + (hh + tt) % 2

    def owner(band):
        tt = band // 2
        return (band % 2 + tt) % 2, tt

    def dev(qq, hh, tt):
        return {"slab": 2 * qq + hh, "term": tt}

    offsets = [(dh, dt) for dh in (1, 0) for dt in range(nt - 1, -1, -1) if (dh, dt) != (0, 0)]

    def partner(sign, dh, dt):
        return (h + dh) % 2, (t + sign * dt + nt) % nt

    barrier = pltpu.get_barrier_semaphore()
    for dh, dt in offsets:
        hh, tt = partner(1, dh, dt)
        pl.semaphore_signal(barrier, inc=1, device_id=dev(q, hh, tt), device_id_type=pl.DeviceIdType.MESH)

    @pl.when(q > 0)
    def _():
        pl.semaphore_signal(barrier, inc=1, device_id=dev(q - 1, h, t), device_id_type=pl.DeviceIdType.MESH)

    @pl.when(q < pairs - 1)
    def _():
        pl.semaphore_signal(barrier, inc=1, device_id=dev(q + 1, h, t), device_id_type=pl.DeviceIdType.MESH)

    below = (q + pairs - 1) // pairs
    above = (2 * pairs - 2 - q) // pairs
    pl.semaphore_wait(barrier, len(offsets) + below + above)

    def remote(src, dst, send, recv, device):
        return pltpu.make_async_remote_copy(
            src_ref=src, dst_ref=dst, send_sem=send, recv_sem=recv,
            device_id=device, device_id_type=pl.DeviceIdType.MESH,
        )

    def band_rows(band):
        return pl.ds(pl.multiple_of(band * rb, 8), rb)

    def b_pair(part, band):
        plane = h if part == 0 else 1 - h
        src = b_hbm.at[:, plane, band_rows(band), :]
        dst = bufb.at[pl.ds(t * tp, tp), 1 + 2 * h + plane, pl.ds(first, rb), :]
        return src, dst

    b_copies = []
    for part in range(2):
        for n, (dh, dt) in enumerate(offsets):
            hh, tt = partner(1, dh, dt)
            src, dst = b_pair(part, band_of(hh, tt))
            slot = part * len(offsets) + n
            copy = remote(src, dst, b_send.at[slot], b_recv.at[slot], dev(q, hh, tt))
            copy.start()
            b_copies.append(copy)
    own_b = [pltpu.make_async_copy(*b_pair(part, g), local_sem.at[part]) for part in range(2)]
    for copy in own_b:
        copy.start()

    def half(hh):
        return pl.ds(pl.multiple_of(rb * ((hh + t) % 2), 8), rb)

    my_planes = pl.ds(h * 2, 2)
    other = dev(q, 1 - h, t)
    c_copies = [
        remote(cond_hbm.at[:, :, half(1 - h), :], cond.at[pl.ds(0, DIM), my_planes], c_send.at[0], c_recv.at[0], other),
        remote(mean_hbm.at[:, half(1 - h), :], cond.at[DIM, my_planes], c_send.at[1], c_recv.at[1], other),
    ]
    own_c = [
        pltpu.make_async_copy(cond_hbm.at[:, :, half(h), :], cond.at[pl.ds(0, DIM), my_planes], local_sem.at[2]),
        pltpu.make_async_copy(mean_hbm.at[:, half(h), :], cond.at[DIM, my_planes], local_sem.at[3]),
    ]
    for copy in c_copies + own_c:
        copy.start()

    def clear(plane):
        def body(j, carry):
            zero = jnp.zeros((rb, 128), jnp.float32)
            bufb[j, plane, first:last, :] = zero
            bufd[j, plane, first:last, :] = zero
            return carry
        lax.fori_loop(0, terms, body, 0)

    @pl.when(q == 0)
    def _():
        clear(0)

    @pl.when(q == pairs - 1)
    def _():
        clear(5)

    def clear_rows(j, carry):
        zero = jnp.zeros((4, 1, 128), jnp.float32)
        for buf in (bufb, bufd):
            buf[j, 1:5, first - 1:first, :] = zero
            buf[j, 1:5, last:last + 1, :] = zero
        return carry

    lax.fori_loop(0, terms, clear_rows, 0)

    @pl.when(g == 0)
    def _():
        for step in range(2):
            rows_in[step, 0] = jnp.zeros(rows_in.shape[2:], jnp.float32)

    @pl.when(g == bands - 1)
    def _():
        for step in range(2):
            rows_in[step, 1] = jnp.zeros(rows_in.shape[2:], jnp.float32)

    def z_copy(step, buf, hh, part, at, size):
        slot = step * bands + hh * nt + part
        return remote(
            buf.at[pl.ds(at, size), 1 + 3 * hh, pl.ds(first, rb), :],
            buf.at[pl.ds(at, size), 5 * (1 - hh), pl.ds(first, rb), :],
            z_send.at[slot], z_recv.at[slot], dev(q - 1 + 2 * hh, h, t),
        )

    def z_sends(hh):
        target = q - 1 + 2 * hh
        return jnp.logical_and(target >= 0, target < pairs)

    def z_receives(hh):
        source = q + 1 - 2 * hh
        return jnp.logical_and(source >= 0, source < pairs)

    def forward(hh, tt):
        @pl.when(z_sends(hh))
        def _():
            z_copy(0, bufb, hh, tt, tt * tp, tp).start()

    def row_copies(step, part):
        up_h, up_t = owner(lax.rem(g + bands - 1, bands))
        down_h, down_t = owner(lax.rem(g + 1, bands))
        up = remote(
            rows_out.at[step, 0, part], rows_in.at[step, 1, part],
            r_send.at[step, 0, part], r_recv.at[step, 1, part], dev(q, up_h, up_t))
        down = remote(
            rows_out.at[step, 1, part], rows_in.at[step, 0, part],
            r_send.at[step, 1, part], r_recv.at[step, 0, part], dev(q, down_h, down_t))
        return up, down

    def planes_of(step, part):
        if step == 0:
            return ((0, 3), (1, 2))[part]
        return 2 * part, 2 * part + 1

    def send_rows(step, part, buf):
        planes = planes_of(step, part)

        def body(jt, carry):
            for tt in range(nt):
                for w in range(2):
                    at = 2 * tt + w
                    j = tt * tp + jt
                    rows_out[step, 0, part, jt, at:at + 1, :] = buf[j, planes[w] + 1, first:first + 1, :]
                    rows_out[step, 1, part, jt, at:at + 1, :] = buf[j, planes[w] + 1, last - 1:last, :]
            return carry
        lax.fori_loop(0, tp, body, 0)
        up, down = row_copies(step, part)

        @pl.when(g > 0)
        def _():
            up.start()

        @pl.when(g < bands - 1)
        def _():
            down.start()

    def wait_rows(step):
        for part in range(2):
            up, down = row_copies(step, part)

            @pl.when(g > 0)
            def _():
                down.wait_recv()

            @pl.when(g < bands - 1)
            def _():
                up.wait_recv()

    def end_rows(step):
        for part in range(2):
            up, down = row_copies(step, part)

            @pl.when(g > 0)
            def _():
                up.wait_send()

            @pl.when(g < bands - 1)
            def _():
                down.wait_send()

    def laplacian(buf):
        lane = lax.broadcasted_iota(jnp.int32, (4, rb, 128), 2)

        def body(jj, carry):
            for a in range(2):
                j = 2 * jj + a
                field = buf[j, 1:5, first:last, :]
                beside = buf[j, 2:6, first:last, :] + buf[j, 0:4, first:last, :]
                beside = beside + buf[j, 1:5, first + 1:last + 1, :] + buf[j, 1:5, first - 1:last - 1, :]
                after = jnp.where(lane == 127, 0.0, pltpu.roll(field, 127, 2))
                before = jnp.where(lane == 0, 0.0, pltpu.roll(field, 1, 2))
                lap[j] = 6.0 * field - (beside + after + before)
            return carry
        lax.fori_loop(0, terms // 2, body, 0)

    def correct(step):
        def body(jt, carry):
            for part in range(2):
                planes = planes_of(step, part)
                for tt in range(nt):
                    for w in range(2):
                        at = 2 * tt + w
                        j = tt * tp + jt
                        p = planes[w]
                        lap[j, p, 0:1, :] = lap[j, p, 0:1, :] - rows_in[step, 0, part, jt, at:at + 1, :]
                        lap[j, p, rb - 1:rb, :] = lap[j, p, rb - 1:rb, :] - rows_in[step, 1, part, jt, at:at + 1, :]
            return carry
        lax.fori_loop(0, tp, body, 0)

    table = galerkin_entries(DIM, DEG)

    def coupled(hh, finish):
        def body(w, carry):
            p = 2 * hh + w
            factors = [cond[k, p] for k in range(DIM)]
            mean = cond[DIM, p]
            for i in range(terms):
                total = mean * lap[i, p]
                for k in range(DIM):
                    mixed = None
                    for col, value in table[i][k]:
                        part = value * lap[col, p]
                        mixed = part if mixed is None else mixed + part
                    if mixed is not None:
                        total = total + factors[k] * mixed
                finish(i, p, total)
            return carry
        lax.fori_loop(0, 2, body, 0)

    center = 0.5 * (upper_edge + lower_edge)
    half_width = 0.5 * (upper_edge - lower_edge)
    sigma = center / half_width
    rho = 1.0 / sigma
    rho_next = 1.0 / (2.0 * sigma - rho)

    def finish_first(i, p, total):
        b = bufb[i, p + 1, first:last, :]
        residual = b - (1.0 / center) * total
        start = (1.0 / center) * b
        direction = (rho_next * rho) * start + (2.0 * rho_next / half_width) * residual
        r1[i, p] = residual
        bufd[i, p + 1, first:last, :] = direction
        sol[i, p] = start + direction

    def finish_second(i, p, total):
        r1[i, p] = r1[i, p] - total

    out_copies = []
    own_out = []

    def send_half(which, dh, src, dst):
        for n, (dh_n, dt) in enumerate(offsets):
            if dh_n == dh:
                hh, tt = partner(1, dh, dt)
                slot = which * len(offsets) + n
                copy = remote(
                    src.at[pl.ds(tt * tp, tp), pl.ds(hh * 2, 2)],
                    dst.at[:, :, band_rows(g), :],
                    o_send.at[slot], o_recv.at[slot], dev(q, hh, tt),
                )
                copy.start()
                out_copies.append(copy)
        if dh == 0:
            copy = pltpu.make_async_copy(
                src.at[pl.ds(t * tp, tp), pl.ds(h * 2, 2)], dst.at[:, :, band_rows(g), :], local_sem.at[4 + which])
            copy.start()
            own_out.append(copy)

    for part in range(2):
        own_b[part].wait()
        if part == 0:
            forward(h, t)
        for n, (dh, dt) in enumerate(offsets):
            b_copies[part * len(offsets) + n].wait_recv()
            if part == 0:
                hh, tt = partner(-1, dh, dt)
                forward(hh, tt)
        send_rows(0, part, bufb)
    for hh in range(2):
        @pl.when(z_receives(hh))
        def _(hh=hh):
            for tt in range(nt):
                z_copy(0, bufb, hh, tt, tt * tp, tp).wait_recv()
    laplacian(bufb)
    for copy in own_c:
        copy.wait()
    for copy in c_copies:
        copy.wait()
    wait_rows(0)
    correct(0)
    for dh in (1, 0):
        hh = (h + dh) % 2
        coupled(hh, finish_first)
        send_rows(1, hh, bufd)

        @pl.when(z_sends(hh))
        def _(hh=hh):
            z_copy(1, bufd, hh, 0, 0, terms).start()
        send_half(0, dh, sol, sol_hbm)

    for hh in range(2):
        @pl.when(z_receives(hh))
        def _(hh=hh):
            z_copy(1, bufd, hh, 0, 0, terms).wait_recv()
    laplacian(bufd)
    wait_rows(1)
    correct(1)
    for dh in (1, 0):
        coupled((h + dh) % 2, finish_second)
        send_half(1, dh, r1, res_hbm)

    for copy in b_copies:
        copy.wait_send()
    for step in range(2):
        end_rows(step)
    for hh in range(2):
        @pl.when(z_sends(hh))
        def _(hh=hh):
            for tt in range(nt):
                z_copy(0, bufb, hh, tt, tt * tp, tp).wait_send()
            z_copy(1, bufd, hh, 0, 0, terms).wait_send()
    for copy in own_out:
        copy.wait()
    for copy in out_copies:
        copy.wait()


def solution(mesh):
    slabs, nt = mesh.shape["slab"], mesh.shape["term"]

    def shards(right_side, mean_cond, cond_terms):
        tp, zp, ny, nx = right_side.shape
        assert zp == 2
        terms = tp * nt
        rb = ny // (2 * nt)
        partners = 2 * nt - 1
        return pl.pallas_call(
            functools.partial(kernel, (slabs, nt, tp, rb, terms)),
            out_shape=[jax.ShapeDtypeStruct(right_side.shape, jnp.float32)] * 2,
            in_specs=[pl.BlockSpec(memory_space=pltpu.HBM)] * 3,
            out_specs=[pl.BlockSpec(memory_space=pl.ANY)] * 2,
            scratch_shapes=[
                pltpu.VMEM((terms, 6, rb + 16, nx), jnp.float32),
                pltpu.VMEM((terms, 6, rb + 16, nx), jnp.float32),
                pltpu.VMEM((terms, 4, rb, nx), jnp.float32),
                pltpu.VMEM((terms, 4, rb, nx), jnp.float32),
                pltpu.VMEM((terms, 4, rb, nx), jnp.float32),
                pltpu.VMEM((DIM + 1, 4, rb, nx), jnp.float32),
                pltpu.VMEM((2, 2, 2, tp, 2 * nt, nx), jnp.float32),
                pltpu.VMEM((2, 2, 2, tp, 2 * nt, nx), jnp.float32),
                pltpu.SemaphoreType.DMA((6,)),
                pltpu.SemaphoreType.DMA((2 * partners,)),
                pltpu.SemaphoreType.DMA((2 * partners,)),
                pltpu.SemaphoreType.DMA((2,)),
                pltpu.SemaphoreType.DMA((2,)),
                pltpu.SemaphoreType.DMA((4 * nt,)),
                pltpu.SemaphoreType.DMA((4 * nt,)),
                pltpu.SemaphoreType.DMA((2, 2, 2)),
                pltpu.SemaphoreType.DMA((2, 2, 2)),
                pltpu.SemaphoreType.DMA((2 * partners,)),
                pltpu.SemaphoreType.DMA((2 * partners,)),
            ],
            compiler_params=pltpu.CompilerParams(
                collective_id=0, has_side_effects=True, vmem_limit_bytes=48 * 2**20
            ),
        )(right_side, mean_cond, cond_terms)

    placed = (P("term", "slab", None, None), P("slab", "term", None), P(None, "slab", "term", None))
    return jax.shard_map(
        shards,
        mesh=mesh,
        in_specs=placed,
        out_specs=(P("term", "slab", None, None), P("term", "slab", None, None)),
        check_vma=False,
    )
```

```python
import functools
import math

import jax
import jax.numpy as jnp
from jax import lax
from jax.experimental import pallas as pl
from jax.experimental.pallas import tpu as pltpu
from jax.sharding import PartitionSpec as P

DIM = 6
DEG = 3
ITERS = 2

lower_edge = 2.0
upper_edge = 72.0


def compositions(degree_sum, slots_left):
    if slots_left == 1:
        return [[degree_sum]]
    listing = []
    for leading in range(degree_sum, -1, -1):
        for remainder in compositions(degree_sum - leading, slots_left - 1):
            listing.append([leading] + remainder)
    return listing


def galerkin_entries(variables, degree):
    indices = []
    for degree_level in range(degree + 1):
        indices.extend(tuple(c) for c in compositions(degree_level, variables))
    place = {index: i for i, index in enumerate(indices)}
    rows = []
    for index in indices:
        per_variable = []
        for variable in range(variables):
            entries = []
            for step in (-1, 1):
                other = list(index)
                other[variable] += step
                col = place.get(tuple(other))
                if col is not None:
                    higher = max(index[variable], other[variable])
                    entries.append((col, higher / math.sqrt(4.0 * higher * higher - 1.0)))
            per_variable.append(entries)
        rows.append(per_variable)
    return rows


def kernel(
    dims,
    b_hbm, mean_hbm, cond_hbm,
    sol_hbm, res_hbm,
    bufb, bufd, lap, r1, sol, cond,
    rows_out, rows_in,
    local_sem, b_send, b_recv, c_send, c_recv, z_send, z_recv, r_send, r_recv, o_send, o_recv,
):
    slabs, nt, tp, rb, terms = dims
    pairs = slabs // 2
    bands = 2 * nt
    first, last = 8, 8 + rb
    s = lax.axis_index("slab")
    t = lax.axis_index("term")
    q = s // 2
    h = s % 2
    g = 2 * t + (h + t) % 2

    def band_of(hh, tt):
        return 2 * tt + (hh + tt) % 2

    def owner(band):
        tt = band // 2
        return (band % 2 + tt) % 2, tt

    def dev(qq, hh, tt):
        return {"slab": 2 * qq + hh, "term": tt}

    u, c = t // 2, t % 2
    offsets = [
        (1 - c, c, 0), (c, 1 - c, 0), (1 - c, c, 1), (c, 1 - c, 1),
        (1, 1, 0), (1, 1, 1), (0, 0, 1),
    ]

    def partner(dh, du, dc):
        return (h + dh) % 2, 2 * ((u + du) % 2) + (c + dc) % 2

    def slot_of(round_, dh, du, dc):
        return len(offsets) * round_ + 4 * dh + 2 * du + dc - 1

    barrier = pltpu.get_barrier_semaphore()
    for offset in offsets:
        hh, tt = partner(*offset)
        pl.semaphore_signal(barrier, inc=1, device_id=dev(q, hh, tt), device_id_type=pl.DeviceIdType.MESH)

    @pl.when(q > 0)
    def _():
        pl.semaphore_signal(barrier, inc=1, device_id=dev(q - 1, h, t), device_id_type=pl.DeviceIdType.MESH)

    @pl.when(q < pairs - 1)
    def _():
        pl.semaphore_signal(barrier, inc=1, device_id=dev(q + 1, h, t), device_id_type=pl.DeviceIdType.MESH)

    below = (q + pairs - 1) // pairs
    above = (2 * pairs - 2 - q) // pairs
    pl.semaphore_wait(barrier, len(offsets) + below + above)

    def remote(src, dst, send, recv, device):
        return pltpu.make_async_remote_copy(
            src_ref=src, dst_ref=dst, send_sem=send, recv_sem=recv,
            device_id=device, device_id_type=pl.DeviceIdType.MESH,
        )

    def band_rows(band):
        return pl.ds(pl.multiple_of(band * rb, 8), rb)

    def b_pair(part, band):
        plane = h if part == 0 else 1 - h
        src = b_hbm.at[:, plane, band_rows(band), :]
        dst = bufb.at[pl.ds(t * tp, tp), 1 + 2 * h + plane, pl.ds(first, rb), :]
        return src, dst

    b_copies = []
    for part in range(2):
        for offset in offsets:
            hh, tt = partner(*offset)
            src, dst = b_pair(part, band_of(hh, tt))
            slot = slot_of(part, *offset)
            copy = remote(src, dst, b_send.at[slot], b_recv.at[slot], dev(q, hh, tt))
            copy.start()
            b_copies.append(copy)
    own_b = [pltpu.make_async_copy(*b_pair(part, g), local_sem.at[part]) for part in range(2)]
    for copy in own_b:
        copy.start()

    def half(hh):
        return pl.ds(pl.multiple_of(rb * ((hh + t) % 2), 8), rb)

    my_planes = pl.ds(h * 2, 2)
    other = dev(q, 1 - h, t)
    c_copies = [
        remote(cond_hbm.at[:, :, half(1 - h), :], cond.at[pl.ds(0, DIM), my_planes], c_send.at[0], c_recv.at[0], other),
        remote(mean_hbm.at[:, half(1 - h), :], cond.at[DIM, my_planes], c_send.at[1], c_recv.at[1], other),
    ]
    own_c = [
        pltpu.make_async_copy(cond_hbm.at[:, :, half(h), :], cond.at[pl.ds(0, DIM), my_planes], local_sem.at[2]),
        pltpu.make_async_copy(mean_hbm.at[:, half(h), :], cond.at[DIM, my_planes], local_sem.at[3]),
    ]
    for copy in c_copies + own_c:
        copy.start()

    def clear(plane):
        def body(j, carry):
            zero = jnp.zeros((rb, 128), jnp.float32)
            bufb[j, plane, first:last, :] = zero
            bufd[j, plane, first:last, :] = zero
            return carry
        lax.fori_loop(0, terms, body, 0)

    @pl.when(q == 0)
    def _():
        clear(0)

    @pl.when(q == pairs - 1)
    def _():
        clear(5)

    def clear_rows(j, carry):
        zero = jnp.zeros((4, 1, 128), jnp.float32)
        for buf in (bufb, bufd):
            buf[j, 1:5, first - 1:first, :] = zero
            buf[j, 1:5, last:last + 1, :] = zero
        return carry

    lax.fori_loop(0, terms, clear_rows, 0)

    @pl.when(g == 0)
    def _():
        for step in range(2):
            rows_in[step, 0] = jnp.zeros(rows_in.shape[2:], jnp.float32)

    @pl.when(g == bands - 1)
    def _():
        for step in range(2):
            rows_in[step, 1] = jnp.zeros(rows_in.shape[2:], jnp.float32)

    def z_copy(step, buf, hh, part, at, size):
        slot = step * bands + hh * nt + part
        return remote(
            buf.at[pl.ds(at, size), 1 + 3 * hh, pl.ds(first, rb), :],
            buf.at[pl.ds(at, size), 5 * (1 - hh), pl.ds(first, rb), :],
            z_send.at[slot], z_recv.at[slot], dev(q - 1 + 2 * hh, h, t),
        )

    def z_sends(hh):
        target = q - 1 + 2 * hh
        return jnp.logical_and(target >= 0, target < pairs)

    def z_receives(hh):
        source = q + 1 - 2 * hh
        return jnp.logical_and(source >= 0, source < pairs)

    def forward(hh, tt):
        @pl.when(z_sends(hh))
        def _():
            z_copy(0, bufb, hh, tt, tt * tp, tp).start()

    def row_copies(step, part):
        up_h, up_t = owner(lax.rem(g + bands - 1, bands))
        down_h, down_t = owner(lax.rem(g + 1, bands))
        up = remote(
            rows_out.at[step, 0, part], rows_in.at[step, 1, part],
            r_send.at[step, 0, part], r_recv.at[step, 1, part], dev(q, up_h, up_t))
        down = remote(
            rows_out.at[step, 1, part], rows_in.at[step, 0, part],
            r_send.at[step, 1, part], r_recv.at[step, 0, part], dev(q, down_h, down_t))
        return up, down

    def planes_of(step, part):
        if step == 0:
            return ((0, 3), (1, 2))[part]
        return 2 * part, 2 * part + 1

    def send_rows(step, part, buf):
        planes = planes_of(step, part)

        def body(jt, carry):
            for tt in range(nt):
                for w in range(2):
                    at = 2 * tt + w
                    j = tt * tp + jt
                    rows_out[step, 0, part, jt, at:at + 1, :] = buf[j, planes[w] + 1, first:first + 1, :]
                    rows_out[step, 1, part, jt, at:at + 1, :] = buf[j, planes[w] + 1, last - 1:last, :]
            return carry
        lax.fori_loop(0, tp, body, 0)
        up, down = row_copies(step, part)

        @pl.when(g > 0)
        def _():
            up.start()

        @pl.when(g < bands - 1)
        def _():
            down.start()

    def wait_rows(step):
        for part in range(2):
            up, down = row_copies(step, part)

            @pl.when(g > 0)
            def _():
                down.wait_recv()

            @pl.when(g < bands - 1)
            def _():
                up.wait_recv()

    def end_rows(step):
        for part in range(2):
            up, down = row_copies(step, part)

            @pl.when(g > 0)
            def _():
                up.wait_send()

            @pl.when(g < bands - 1)
            def _():
                down.wait_send()

    lane = lax.broadcasted_iota(jnp.int32, (rb, 128), 1)

    def lateral(buf, j, plane):
        field = buf[j, plane, first:last, :]
        beside = buf[j, plane, first + 1:last + 1, :] + buf[j, plane, first - 1:last - 1, :]
        after = jnp.where(lane == 127, 0.0, pltpu.roll(field, 127, 1))
        before = jnp.where(lane == 0, 0.0, pltpu.roll(field, 1, 1))
        return 6.0 * field - (beside + after + before)

    def laplacian_outer(buf):
        def body(jj, carry):
            for a in range(2):
                j = 2 * jj + a
                lap[j, 0] = lateral(buf, j, 1)
                lap[j, 3] = lateral(buf, j, 4)
            return carry
        lax.fori_loop(0, terms // 2, body, 0)

    def laplacian_rest(buf):
        def body(jj, carry):
            for a in range(2):
                j = 2 * jj + a
                planes = [buf[j, p, first:last, :] for p in range(6)]
                lap[j, 0] = lap[j, 0] - (planes[0] + planes[2])
                lap[j, 1] = lateral(buf, j, 2) - (planes[1] + planes[3])
                lap[j, 2] = lateral(buf, j, 3) - (planes[2] + planes[4])
                lap[j, 3] = lap[j, 3] - (planes[3] + planes[5])
            return carry
        lax.fori_loop(0, terms // 2, body, 0)

    def correct(step):
        def body(jt, carry):
            for part in range(2):
                planes = planes_of(step, part)
                for tt in range(nt):
                    for w in range(2):
                        at = 2 * tt + w
                        j = tt * tp + jt
                        p = planes[w]
                        lap[j, p, 0:1, :] = lap[j, p, 0:1, :] - rows_in[step, 0, part, jt, at:at + 1, :]
                        lap[j, p, rb - 1:rb, :] = lap[j, p, rb - 1:rb, :] - rows_in[step, 1, part, jt, at:at + 1, :]
            return carry
        lax.fori_loop(0, tp, body, 0)

    table = galerkin_entries(DIM, DEG)

    def coupled(hh, finish):
        def body(w, carry):
            p = 2 * hh + w
            factors = [cond[k, p] for k in range(DIM)]
            mean = cond[DIM, p]
            for i in range(terms):
                total = mean * lap[i, p]
                for k in range(DIM):
                    mixed = None
                    for col, value in table[i][k]:
                        part = value * lap[col, p]
                        mixed = part if mixed is None else mixed + part
                    if mixed is not None:
                        total = total + factors[k] * mixed
                finish(i, p, total)
            return carry
        lax.fori_loop(0, 2, body, 0)

    center = 0.5 * (upper_edge + lower_edge)
    half_width = 0.5 * (upper_edge - lower_edge)
    sigma = center / half_width
    rho = 1.0 / sigma
    rho_next = 1.0 / (2.0 * sigma - rho)

    def finish_first(i, p, total):
        b = bufb[i, p + 1, first:last, :]
        residual = b - (1.0 / center) * total
        start = (1.0 / center) * b
        direction = (rho_next * rho) * start + (2.0 * rho_next / half_width) * residual
        r1[i, p] = residual
        bufd[i, p + 1, first:last, :] = direction
        sol[i, p] = start + direction

    def finish_second(i, p, total):
        r1[i, p] = r1[i, p] - total

    out_copies = []
    own_out = []

    def send_out(which, src, dst):
        for offset in offsets:
            hh, tt = partner(*offset)
            slot = slot_of(which, *offset)
            copy = remote(
                src.at[pl.ds(tt * tp, tp), pl.ds(hh * 2, 2)],
                dst.at[:, :, band_rows(g), :],
                o_send.at[slot], o_recv.at[slot], dev(q, hh, tt),
            )
            copy.start()
            out_copies.append(copy)
        copy = pltpu.make_async_copy(
            src.at[pl.ds(t * tp, tp), pl.ds(h * 2, 2)], dst.at[:, :, band_rows(g), :], local_sem.at[4 + which])
        copy.start()
        own_out.append(copy)

    for part in range(2):
        own_b[part].wait()
        if part == 0:
            forward(h, t)
        for n in [6, 0, 1, 2, 3, 4, 5]:
            b_copies[part * len(offsets) + n].wait_recv()
            if part == 0:
                forward(*partner(*offsets[n]))
        send_rows(0, part, bufb)
        if part == 0:
            laplacian_outer(bufb)
    for hh in range(2):
        @pl.when(z_receives(hh))
        def _(hh=hh):
            for tt in range(nt):
                z_copy(0, bufb, hh, tt, tt * tp, tp).wait_recv()
    laplacian_rest(bufb)
    for copy in own_c:
        copy.wait()
    for copy in c_copies:
        copy.wait()
    wait_rows(0)
    correct(0)
    for dh in (1, 0):
        hh = (h + dh) % 2
        coupled(hh, finish_first)
        send_rows(1, hh, bufd)

        @pl.when(z_sends(hh))
        def _(hh=hh):
            z_copy(1, bufd, hh, 0, 0, terms).start()
    send_out(0, sol, sol_hbm)
    laplacian_outer(bufd)

    for hh in range(2):
        @pl.when(z_receives(hh))
        def _(hh=hh):
            z_copy(1, bufd, hh, 0, 0, terms).wait_recv()
    laplacian_rest(bufd)
    wait_rows(1)
    correct(1)
    for dh in (1, 0):
        coupled((h + dh) % 2, finish_second)
    send_out(1, r1, res_hbm)

    for copy in b_copies:
        copy.wait_send()
    for step in range(2):
        end_rows(step)
    for hh in range(2):
        @pl.when(z_sends(hh))
        def _(hh=hh):
            for tt in range(nt):
                z_copy(0, bufb, hh, tt, tt * tp, tp).wait_send()
            z_copy(1, bufd, hh, 0, 0, terms).wait_send()
    for copy in own_out:
        copy.wait()
    for copy in out_copies:
        copy.wait()


def solution(mesh):
    slabs, nt = mesh.shape["slab"], mesh.shape["term"]

    def shards(right_side, mean_cond, cond_terms):
        tp, zp, ny, nx = right_side.shape
        assert zp == 2 and nt == 4
        terms = tp * nt
        rb = ny // (2 * nt)
        partners = 2 * nt - 1
        return pl.pallas_call(
            functools.partial(kernel, (slabs, nt, tp, rb, terms)),
            out_shape=[jax.ShapeDtypeStruct(right_side.shape, jnp.float32)] * 2,
            in_specs=[pl.BlockSpec(memory_space=pltpu.HBM)] * 3,
            out_specs=[pl.BlockSpec(memory_space=pl.ANY)] * 2,
            scratch_shapes=[
                pltpu.VMEM((terms, 6, rb + 16, nx), jnp.float32),
                pltpu.VMEM((terms, 6, rb + 16, nx), jnp.float32),
                pltpu.VMEM((terms, 4, rb, nx), jnp.float32),
                pltpu.VMEM((terms, 4, rb, nx), jnp.float32),
                pltpu.VMEM((terms, 4, rb, nx), jnp.float32),
                pltpu.VMEM((DIM + 1, 4, rb, nx), jnp.float32),
                pltpu.VMEM((2, 2, 2, tp, 2 * nt, nx), jnp.float32),
                pltpu.VMEM((2, 2, 2, tp, 2 * nt, nx), jnp.float32),
                pltpu.SemaphoreType.DMA((6,)),
                pltpu.SemaphoreType.DMA((2 * partners,)),
                pltpu.SemaphoreType.DMA((2 * partners,)),
                pltpu.SemaphoreType.DMA((2,)),
                pltpu.SemaphoreType.DMA((2,)),
                pltpu.SemaphoreType.DMA((4 * nt,)),
                pltpu.SemaphoreType.DMA((4 * nt,)),
                pltpu.SemaphoreType.DMA((2, 2, 2)),
                pltpu.SemaphoreType.DMA((2, 2, 2)),
                pltpu.SemaphoreType.DMA((2 * partners,)),
                pltpu.SemaphoreType.DMA((2 * partners,)),
            ],
            compiler_params=pltpu.CompilerParams(
                collective_id=0, has_side_effects=True, vmem_limit_bytes=48 * 2**20
            ),
        )(right_side, mean_cond, cond_terms)

    placed = (P("term", "slab", None, None), P("slab", "term", None), P(None, "slab", "term", None))
    return jax.shard_map(
        shards,
        mesh=mesh,
        in_specs=placed,
        out_specs=(P("term", "slab", None, None), P("term", "slab", None, None)),
        check_vma=False,
    )
```

```python
import functools
import math

import jax
import jax.numpy as jnp
from jax import lax
from jax.experimental import pallas as pl
from jax.experimental.pallas import tpu as pltpu
from jax.sharding import PartitionSpec as P

DIM = 6
DEG = 3
ITERS = 2

lower_edge = 2.0
upper_edge = 72.0


def compositions(degree_sum, slots_left):
    if slots_left == 1:
        return [[degree_sum]]
    listing = []
    for leading in range(degree_sum, -1, -1):
        for remainder in compositions(degree_sum - leading, slots_left - 1):
            listing.append([leading] + remainder)
    return listing


def galerkin_entries(variables, degree):
    indices = []
    for degree_level in range(degree + 1):
        indices.extend(tuple(c) for c in compositions(degree_level, variables))
    place = {index: i for i, index in enumerate(indices)}
    rows = []
    for index in indices:
        per_variable = []
        for variable in range(variables):
            entries = []
            for step in (-1, 1):
                other = list(index)
                other[variable] += step
                col = place.get(tuple(other))
                if col is not None:
                    higher = max(index[variable], other[variable])
                    entries.append((col, higher / math.sqrt(4.0 * higher * higher - 1.0)))
            per_variable.append(entries)
        rows.append(per_variable)
    return rows


def kernel(
    dims,
    b_hbm, mean_hbm, cond_hbm,
    sol_hbm, res_hbm,
    bufb, bufd, lap, r1, sol, cond,
    rows_out, rows_in,
    local_sem, b_send, b_recv, c_send, c_recv, z_send, z_recv, r_send, r_recv, o_send, o_recv,
):
    slabs, nt, tp, rb, terms = dims
    pairs = slabs // 2
    bands = 2 * nt
    first, last = 8, 8 + rb
    s = lax.axis_index("slab")
    t = lax.axis_index("term")
    q = s // 2
    h = s % 2
    g = 2 * t + (h + t) % 2

    def band_of(hh, tt):
        return 2 * tt + (hh + tt) % 2

    def owner(band):
        tt = band // 2
        return (band % 2 + tt) % 2, tt

    def dev(qq, hh, tt):
        return {"slab": 2 * qq + hh, "term": tt}

    u, c = t // 2, t % 2
    offsets = [
        (1 - c, c, 0), (c, 1 - c, 0), (1 - c, c, 1), (c, 1 - c, 1),
        (1, 1, 0), (1, 1, 1), (0, 0, 1),
    ]

    def partner(dh, du, dc):
        return (h + dh) % 2, 2 * ((u + du) % 2) + (c + dc) % 2

    def slot_of(round_, dh, du, dc):
        return len(offsets) * round_ + 4 * dh + 2 * du + dc - 1

    barrier = pltpu.get_barrier_semaphore()
    for offset in offsets:
        hh, tt = partner(*offset)
        pl.semaphore_signal(barrier, inc=1, device_id=dev(q, hh, tt), device_id_type=pl.DeviceIdType.MESH)

    @pl.when(q > 0)
    def _():
        pl.semaphore_signal(barrier, inc=1, device_id=dev(q - 1, h, t), device_id_type=pl.DeviceIdType.MESH)

    @pl.when(q < pairs - 1)
    def _():
        pl.semaphore_signal(barrier, inc=1, device_id=dev(q + 1, h, t), device_id_type=pl.DeviceIdType.MESH)

    below = (q + pairs - 1) // pairs
    above = (2 * pairs - 2 - q) // pairs
    pl.semaphore_wait(barrier, len(offsets) + below + above)

    def remote(src, dst, send, recv, device):
        return pltpu.make_async_remote_copy(
            src_ref=src, dst_ref=dst, send_sem=send, recv_sem=recv,
            device_id=device, device_id_type=pl.DeviceIdType.MESH,
        )

    def band_rows(band):
        return pl.ds(pl.multiple_of(band * rb, 8), rb)

    def b_pair(part, band):
        plane = h if part == 0 else 1 - h
        src = b_hbm.at[:, plane, band_rows(band), :]
        dst = bufb.at[pl.ds(t * tp, tp), 1 + 2 * h + plane, pl.ds(first, rb), :]
        return src, dst

    b_copies = []
    for part in range(2):
        for offset in offsets:
            hh, tt = partner(*offset)
            src, dst = b_pair(part, band_of(hh, tt))
            slot = slot_of(part, *offset)
            copy = remote(src, dst, b_send.at[slot], b_recv.at[slot], dev(q, hh, tt))
            copy.start()
            b_copies.append(copy)
    own_b = [pltpu.make_async_copy(*b_pair(part, g), local_sem.at[part]) for part in range(2)]
    for copy in own_b:
        copy.start()

    def half(hh):
        return pl.ds(pl.multiple_of(rb * ((hh + t) % 2), 8), rb)

    my_planes = pl.ds(h * 2, 2)
    other = dev(q, 1 - h, t)
    c_copies = [
        remote(cond_hbm.at[:, :, half(1 - h), :], cond.at[pl.ds(0, DIM), my_planes], c_send.at[0], c_recv.at[0], other),
        remote(mean_hbm.at[:, half(1 - h), :], cond.at[DIM, my_planes], c_send.at[1], c_recv.at[1], other),
    ]
    own_c = [
        pltpu.make_async_copy(cond_hbm.at[:, :, half(h), :], cond.at[pl.ds(0, DIM), my_planes], local_sem.at[2]),
        pltpu.make_async_copy(mean_hbm.at[:, half(h), :], cond.at[DIM, my_planes], local_sem.at[3]),
    ]
    for copy in c_copies + own_c:
        copy.start()

    def clear(plane):
        def body(j, carry):
            zero = jnp.zeros((rb, 128), jnp.float32)
            bufb[j, plane, first:last, :] = zero
            bufd[j, plane, first:last, :] = zero
            return carry
        lax.fori_loop(0, terms, body, 0)

    @pl.when(q == 0)
    def _():
        clear(0)

    @pl.when(q == pairs - 1)
    def _():
        clear(5)

    def clear_rows(j, carry):
        zero = jnp.zeros((4, 1, 128), jnp.float32)
        for buf in (bufb, bufd):
            buf[j, 1:5, first - 1:first, :] = zero
            buf[j, 1:5, last:last + 1, :] = zero
        return carry

    lax.fori_loop(0, terms, clear_rows, 0)

    @pl.when(g == 0)
    def _():
        for step in range(2):
            rows_in[step, 0] = jnp.zeros(rows_in.shape[2:], jnp.float32)

    @pl.when(g == bands - 1)
    def _():
        for step in range(2):
            rows_in[step, 1] = jnp.zeros(rows_in.shape[2:], jnp.float32)

    def z_copy(step, buf, hh, part, at, size):
        slot = step * bands + hh * nt + part
        return remote(
            buf.at[pl.ds(at, size), 1 + 3 * hh, pl.ds(first, rb), :],
            buf.at[pl.ds(at, size), 5 * (1 - hh), pl.ds(first, rb), :],
            z_send.at[slot], z_recv.at[slot], dev(q - 1 + 2 * hh, h, t),
        )

    def z_sends(hh):
        target = q - 1 + 2 * hh
        return jnp.logical_and(target >= 0, target < pairs)

    def z_receives(hh):
        source = q + 1 - 2 * hh
        return jnp.logical_and(source >= 0, source < pairs)

    def forward(hh, tt):
        @pl.when(z_sends(hh))
        def _():
            z_copy(0, bufb, hh, tt, tt * tp, tp).start()

    def row_copies(step, part):
        up_h, up_t = owner(lax.rem(g + bands - 1, bands))
        down_h, down_t = owner(lax.rem(g + 1, bands))
        up = remote(
            rows_out.at[step, 0, part], rows_in.at[step, 1, part],
            r_send.at[step, 0, part], r_recv.at[step, 1, part], dev(q, up_h, up_t))
        down = remote(
            rows_out.at[step, 1, part], rows_in.at[step, 0, part],
            r_send.at[step, 1, part], r_recv.at[step, 0, part], dev(q, down_h, down_t))
        return up, down

    def planes_of(step, part):
        if step == 0:
            return ((0, 3), (1, 2))[part]
        return 2 * part, 2 * part + 1

    def send_rows(step, part, buf):
        planes = planes_of(step, part)

        def body(jt, carry):
            for tt in range(nt):
                for w in range(2):
                    at = 2 * tt + w
                    j = tt * tp + jt
                    rows_out[step, 0, part, jt, at:at + 1, :] = buf[j, planes[w] + 1, first:first + 1, :]
                    rows_out[step, 1, part, jt, at:at + 1, :] = buf[j, planes[w] + 1, last - 1:last, :]
            return carry
        lax.fori_loop(0, tp, body, 0)
        up, down = row_copies(step, part)

        @pl.when(g > 0)
        def _():
            up.start()

        @pl.when(g < bands - 1)
        def _():
            down.start()

    def wait_rows(step):
        for part in range(2):
            up, down = row_copies(step, part)

            @pl.when(g > 0)
            def _():
                down.wait_recv()

            @pl.when(g < bands - 1)
            def _():
                up.wait_recv()

    def end_rows(step):
        for part in range(2):
            up, down = row_copies(step, part)

            @pl.when(g > 0)
            def _():
                up.wait_send()

            @pl.when(g < bands - 1)
            def _():
                down.wait_send()

    lane = lax.broadcasted_iota(jnp.int32, (rb, 128), 1)

    def lateral(buf, j, plane):
        field = buf[j, plane, first:last, :]
        beside = buf[j, plane, first + 1:last + 1, :] + buf[j, plane, first - 1:last - 1, :]
        after = jnp.where(lane == 127, 0.0, pltpu.roll(field, 127, 1))
        before = jnp.where(lane == 0, 0.0, pltpu.roll(field, 1, 1))
        return 6.0 * field - (beside + after + before)

    def laplacian_outer(buf):
        def body(jj, carry):
            for a in range(2):
                j = 2 * jj + a
                lap[j, 0] = lateral(buf, j, 1)
                lap[j, 3] = lateral(buf, j, 4)
            return carry
        lax.fori_loop(0, terms // 2, body, 0)

    def laplacian_rest(buf):
        def body(jj, carry):
            for a in range(2):
                j = 2 * jj + a
                planes = [buf[j, p, first:last, :] for p in range(6)]
                lap[j, 0] = lap[j, 0] - (planes[0] + planes[2])
                lap[j, 1] = lateral(buf, j, 2) - (planes[1] + planes[3])
                lap[j, 2] = lateral(buf, j, 3) - (planes[2] + planes[4])
                lap[j, 3] = lap[j, 3] - (planes[3] + planes[5])
            return carry
        lax.fori_loop(0, terms // 2, body, 0)

    def correct(step):
        def body(jt, carry):
            for part in range(2):
                planes = planes_of(step, part)
                for tt in range(nt):
                    for w in range(2):
                        at = 2 * tt + w
                        j = tt * tp + jt
                        p = planes[w]
                        lap[j, p, 0:1, :] = lap[j, p, 0:1, :] - rows_in[step, 0, part, jt, at:at + 1, :]
                        lap[j, p, rb - 1:rb, :] = lap[j, p, rb - 1:rb, :] - rows_in[step, 1, part, jt, at:at + 1, :]
            return carry
        lax.fori_loop(0, tp, body, 0)

    table = galerkin_entries(DIM, DEG)

    def coupled(hh, finish):
        def body(w, carry):
            p = 2 * hh + w
            factors = [cond[k, p] for k in range(DIM)]
            mean = cond[DIM, p]
            for i in range(terms):
                total = mean * lap[i, p]
                for k in range(DIM):
                    mixed = None
                    for col, value in table[i][k]:
                        part = value * lap[col, p]
                        mixed = part if mixed is None else mixed + part
                    if mixed is not None:
                        total = total + factors[k] * mixed
                finish(i, p, total)
            return carry
        lax.fori_loop(0, 2, body, 0)

    center = 0.5 * (upper_edge + lower_edge)
    half_width = 0.5 * (upper_edge - lower_edge)
    sigma = center / half_width
    rho = 1.0 / sigma
    rho_next = 1.0 / (2.0 * sigma - rho)

    def finish_first(i, p, total):
        b = bufb[i, p + 1, first:last, :]
        residual = b - (1.0 / center) * total
        start = (1.0 / center) * b
        direction = (rho_next * rho) * start + (2.0 * rho_next / half_width) * residual
        r1[i, p] = residual
        bufd[i, p + 1, first:last, :] = direction
        sol[i, p] = start + direction

    def finish_second(i, p, total):
        r1[i, p] = r1[i, p] - total

    out_copies = []
    own_out = []

    halves = ((h + 1 - c) % 2, (h + c) % 2)

    def send_out(which, part, src, dst):
        for n in ((0, 2), (1, 3, 4, 5, 6))[part]:
            offset = offsets[n]
            hh, tt = partner(*offset)
            slot = slot_of(which, *offset)
            copy = remote(
                src.at[pl.ds(tt * tp, tp), pl.ds(hh * 2, 2)],
                dst.at[:, :, band_rows(g), :],
                o_send.at[slot], o_recv.at[slot], dev(q, hh, tt),
            )
            copy.start()
            out_copies.append(copy)
        if part == 1:
            copy = pltpu.make_async_copy(
                src.at[pl.ds(t * tp, tp), pl.ds(h * 2, 2)], dst.at[:, :, band_rows(g), :], local_sem.at[4 + which])
            copy.start()
            own_out.append(copy)

    for part in range(2):
        own_b[part].wait()
        if part == 0:
            forward(h, t)
        for n in [6, 0, 1, 2, 3, 4, 5]:
            b_copies[part * len(offsets) + n].wait_recv()
            if part == 0:
                forward(*partner(*offsets[n]))
        send_rows(0, part, bufb)
        if part == 0:
            laplacian_outer(bufb)
    for hh in range(2):
        @pl.when(z_receives(hh))
        def _(hh=hh):
            for tt in range(nt):
                z_copy(0, bufb, hh, tt, tt * tp, tp).wait_recv()
    laplacian_rest(bufb)
    for copy in own_c:
        copy.wait()
    for copy in c_copies:
        copy.wait()
    wait_rows(0)
    correct(0)
    for part, hh in enumerate(halves):
        coupled(hh, finish_first)
        send_rows(1, hh, bufd)

        @pl.when(z_sends(hh))
        def _(hh=hh):
            z_copy(1, bufd, hh, 0, 0, terms).start()
        send_out(0, part, sol, sol_hbm)
    laplacian_outer(bufd)

    for hh in range(2):
        @pl.when(z_receives(hh))
        def _(hh=hh):
            z_copy(1, bufd, hh, 0, 0, terms).wait_recv()
    laplacian_rest(bufd)
    wait_rows(1)
    correct(1)
    for part, hh in enumerate(halves):
        coupled(hh, finish_second)
        send_out(1, part, r1, res_hbm)

    for copy in b_copies:
        copy.wait_send()
    for step in range(2):
        end_rows(step)
    for hh in range(2):
        @pl.when(z_sends(hh))
        def _(hh=hh):
            for tt in range(nt):
                z_copy(0, bufb, hh, tt, tt * tp, tp).wait_send()
            z_copy(1, bufd, hh, 0, 0, terms).wait_send()
    for copy in own_out:
        copy.wait()
    for copy in out_copies:
        copy.wait()


def solution(mesh):
    slabs, nt = mesh.shape["slab"], mesh.shape["term"]

    def shards(right_side, mean_cond, cond_terms):
        tp, zp, ny, nx = right_side.shape
        assert zp == 2 and nt == 4
        terms = tp * nt
        rb = ny // (2 * nt)
        partners = 2 * nt - 1
        return pl.pallas_call(
            functools.partial(kernel, (slabs, nt, tp, rb, terms)),
            out_shape=[jax.ShapeDtypeStruct(right_side.shape, jnp.float32)] * 2,
            in_specs=[pl.BlockSpec(memory_space=pltpu.HBM)] * 3,
            out_specs=[pl.BlockSpec(memory_space=pl.ANY)] * 2,
            scratch_shapes=[
                pltpu.VMEM((terms, 6, rb + 16, nx), jnp.float32),
                pltpu.VMEM((terms, 6, rb + 16, nx), jnp.float32),
                pltpu.VMEM((terms, 4, rb, nx), jnp.float32),
                pltpu.VMEM((terms, 4, rb, nx), jnp.float32),
                pltpu.VMEM((terms, 4, rb, nx), jnp.float32),
                pltpu.VMEM((DIM + 1, 4, rb, nx), jnp.float32),
                pltpu.VMEM((2, 2, 2, tp, 2 * nt, nx), jnp.float32),
                pltpu.VMEM((2, 2, 2, tp, 2 * nt, nx), jnp.float32),
                pltpu.SemaphoreType.DMA((6,)),
                pltpu.SemaphoreType.DMA((2 * partners,)),
                pltpu.SemaphoreType.DMA((2 * partners,)),
                pltpu.SemaphoreType.DMA((2,)),
                pltpu.SemaphoreType.DMA((2,)),
                pltpu.SemaphoreType.DMA((4 * nt,)),
                pltpu.SemaphoreType.DMA((4 * nt,)),
                pltpu.SemaphoreType.DMA((2, 2, 2)),
                pltpu.SemaphoreType.DMA((2, 2, 2)),
                pltpu.SemaphoreType.DMA((2 * partners,)),
                pltpu.SemaphoreType.DMA((2 * partners,)),
            ],
            compiler_params=pltpu.CompilerParams(
                collective_id=0, has_side_effects=True, vmem_limit_bytes=56 * 2**20
            ),
        )(right_side, mean_cond, cond_terms)

    placed = (P("term", "slab", None, None), P("slab", "term", None), P(None, "slab", "term", None))
    return jax.shard_map(
        shards,
        mesh=mesh,
        in_specs=placed,
        out_specs=(P("term", "slab", None, None), P("term", "slab", None, None)),
        check_vma=False,
    )
```
